32 devices in a mesh: dp: 8 (over z, y), rows: 4 (over x, core).
Axes of the slice: x: 2, y: 2, z: 4, core: 2. Of those that a mesh axis runs over, the one named last changes fastest.
Arguments:
- candidates: bfloat16 [16, 4, 32, 32, 1024], P('dp', None, 'rows'), may hold values from -40 to 40
- winners: int32 [16], P('dp'), may hold values from 0 to 3
- conv_weight: bfloat16 [9216, 512], P('dp'), may hold values from -0.0625 to 0.0625
- conv_bias: float32 [512], replicated, may hold values from -3 to 3
- gamma: float32 [1024], replicated, may hold values from 0.5 to 1.5
- beta: float32 [1024], replicated, may hold values from -3 to 3
- cotangent: bfloat16 [16, 32, 32, 512], P('dp', 'rows'), may hold values from -6 to 6
Outputs:
- output: bfloat16 [16, 32, 32, 512], P('dp', 'rows')
- grad_weight: float32 [9216, 512], P('dp')
- grad_bias: float32 [512], replicated
- grad_gamma: float32 [1024], replicated
- grad_beta: float32 [1024], replicated
The draws below stay inside these ranges and needn't reach their ends.
All inputs are finite; a program needn't handle non-finite values.
Results may differ from the reference program's by a relative error of at most 0.003.
Values may be sent and summed in bfloat16 or wider, within the bound.
A program may use at most 128 MiB of HBM per device.

```python
import math
import jax
import jax.numpy as jnp
from jax import lax

C = 1024
CO = 512
GROUPS = 32
H = 32
WD = 32
NCAND = 4
IMAGES = 16


def draw_candidates(key, part):
    key_noise = jax.random.fold_in(key, 11)
    key_chan = jax.random.fold_in(key, 12)
    key_offset = jax.random.fold_in(key, 13)
    shape = (IMAGES, NCAND, H, WD, C)
    chan_scale = jnp.exp(jax.random.uniform(key_chan, (IMAGES, NCAND, 1, 1, C), jnp.float32, math.log(0.3), math.log(3.0)))
    row_pos = lax.broadcasted_iota(jnp.float32, (1, 1, H, 1, 1), 2) / (H - 1)
    noise = jax.random.truncated_normal(key_noise, -4.0, 4.0, shape, jnp.float32)
    row_rise = jnp.exp(math.log(3.0) * row_pos)
    offset = jnp.clip(0.3 * jax.random.normal(key_offset, (IMAGES, NCAND, 1, 1, C), jnp.float32), -1.0, 1.0)
    values = noise * chan_scale * row_rise + offset
    return values.astype(jnp.bfloat16)


def touch_ends(result, stream_key, low, high):
    extent = result.shape
    spot = [jax.random.randint(jax.random.fold_in(stream_key, axis), (), 0, extent[axis]) for axis in range(len(extent))]
    result = result.at[tuple(spot)].set(low)
    longest = extent.index(max(extent))
    spot[longest] = (spot[longest] + 1) % extent[longest]
    return result.at[tuple(spot)].set(high)


def block_levels(key, dims, split, low, largest):
    loudness = 1.0
    for axis_at, parts in split:
        draws = jax.random.uniform(jax.random.fold_in(jax.random.fold_in(key, 6), axis_at), (parts,), jnp.float32, low / len(split), largest / len(split))
        loudness = loudness * jnp.repeat(jnp.exp(draws), dims[axis_at] // parts).reshape((-1,) + (1,) * (len(dims) - 1 - axis_at))
    return loudness


def centred(rng, dims, scale, limit, pieces=(), held_as=jnp.bfloat16):
    result = jax.random.normal(rng, dims, jnp.float32) * scale
    if len(pieces) > 0:
        result = block_levels(rng, dims, pieces, -0.22, 0.18) * result
    return jnp.clip(result, min=-limit, max=limit).astype(held_as)


def setup_inputs(seed: int = 0) -> dict:
    streams_of = jax.random.split(jax.random.key(seed), 8)
    return {
        "candidates": draw_candidates(jax.random.fold_in(streams_of[7], 71), 0),
        "winners": touch_ends(jax.random.randint(streams_of[1], (IMAGES,), 0, NCAND), jax.random.fold_in(streams_of[1], 1), 0, NCAND - 1).astype(jnp.int32),
        "conv_weight": centred(streams_of[2], (9 * C, CO), (9 * C) ** -0.5, 0.0625, ((0, 8),)),
        "conv_bias": centred(streams_of[3], (CO,), 0.5, 3.0, (), jnp.float32),
        "gamma": jnp.clip(1.0 + 0.1 * jax.random.normal(streams_of[4], (C,), jnp.float32), 0.5, 1.5),
        "beta": centred(streams_of[5], (C,), 0.5, 3.0, (), jnp.float32),
        "cotangent": centred(streams_of[6], (IMAGES, H, WD, CO), 1.0, 6.0, ((0, 8), (1, 4))),
    }


EPSILON = 1e-05

def pick_winner(cand_block, winner):
    picked = cand_block[0]
    for cand_index in range(1, NCAND):
        picked = jnp.where(winner == cand_index, cand_block[cand_index], picked)
    return picked

def reference(candidates, winners, conv_weight, conv_bias, gamma, beta, cotangent):
    grad_scale = float(IMAGES * H * WD) ** (-0.5)
    cell_count = H * WD
    total_count = H * WD * (C // GROUPS)

    def image_step(carried, element):
        weight_sum, bias_sum, gamma_sum, beta_sum = carried
        cand_block, winner, cot_image = element
        picked = pick_winner(cand_block, winner)
        grouped = picked.astype(jnp.float32).reshape(H, WD, GROUPS, C // GROUPS)
        group_mean = lax.optimization_barrier(jnp.sum(grouped, axis=(0, 1, 3))) / total_count
        group_var = lax.optimization_barrier(jnp.sum(grouped * grouped, axis=(0, 1, 3))) / total_count - group_mean * group_mean
        normed = ((grouped - group_mean[:, None]) * lax.rsqrt(group_var + EPSILON)[:, None]).reshape(H, WD, C)
        preact = normed * gamma + beta
        activated = jax.nn.silu(preact).astype(jnp.bfloat16)
        padded = jnp.pad(activated, ((1, 1), (1, 1), (0, 0)))
        patches = jnp.concatenate([padded[1 + shift_row:1 + shift_row + H, 1 + shift_col:1 + shift_col + WD].reshape(cell_count, C) for shift_row in (-1, 0, 1) for shift_col in (-1, 0, 1)], axis=1)
        conv_sum = jnp.dot(patches, conv_weight, preferred_element_type=jnp.float32) + conv_bias
        residual = picked[:, :, :CO].reshape(cell_count, CO).astype(jnp.float32)
        output = (conv_sum + residual).astype(jnp.bfloat16).reshape(H, WD, CO)
        flat_cot = cot_image.reshape(cell_count, CO)
        weight_sum = weight_sum + jnp.dot(patches.T, flat_cot, preferred_element_type=jnp.float32)
        bias_sum = bias_sum + lax.optimization_barrier(jnp.sum(flat_cot.astype(jnp.float32), axis=0))
        cot_pad = jnp.pad(cot_image, ((1, 1), (1, 1), (0, 0)))
        back_grad = jnp.zeros((cell_count, C), jnp.float32)
        tap_index = 0
        for shift_row in (-1, 0, 1):
            for shift_col in (-1, 0, 1):
                shifted = cot_pad[1 - shift_row:1 - shift_row + H, 1 - shift_col:1 - shift_col + WD].reshape(cell_count, CO)
                tap_weight = conv_weight[tap_index * C:(tap_index + 1) * C]
                back_grad = back_grad + jnp.dot(shifted, tap_weight.T, preferred_element_type=jnp.float32)
                tap_index = tap_index + 1
        back_grad = (back_grad * grad_scale).reshape(H, WD, C)
        sigmoid_pre = jax.nn.sigmoid(preact)
        pre_grad = back_grad * sigmoid_pre * (1.0 + preact * (1.0 - sigmoid_pre))
        gamma_sum = gamma_sum + lax.optimization_barrier(jnp.sum(pre_grad * normed, axis=(0, 1)))
        beta_sum = beta_sum + lax.optimization_barrier(jnp.sum(pre_grad, axis=(0, 1)))
        return ((weight_sum, bias_sum, gamma_sum, beta_sum), output)
    initial = (jnp.zeros((9 * C, CO), jnp.float32), jnp.zeros((CO,), jnp.float32), jnp.zeros((C,), jnp.float32), jnp.zeros((C,), jnp.float32))
    finals, output = lax.scan(image_step, initial, (candidates, winners, cotangent))
    weight_sum, bias_sum, gamma_sum, beta_sum = finals
    return (output, weight_sum * grad_scale, bias_sum * grad_scale, gamma_sum, beta_sum)
```

```python
import functools
import math

import jax
import jax.numpy as jnp
from jax import lax
from jax.experimental import pallas as pl
from jax.experimental.pallas import tpu as pltpu
from jax.sharding import PartitionSpec as P

GROUPS = 32


EPSILON = 1e-05


CONV_DIMS = ("NHWC", "HWIO", "NHWC")


CHUNKS = 3


VMEM_BYTES = 48 * 1024 * 1024


MESH = pl.DeviceIdType.MESH


def greet(owners, split):
    dp, rows = lax.axis_index("dp"), lax.axis_index("rows")
    lane, side = dp // 2, dp % 2
    peers = [{"rows": lax.rem(rows + k, split)} for k in range(1, split)]
    peers += [{"dp": lax.rem(dp + k, owners)} for k in range(1, owners)]
    barrier = pltpu.get_barrier_semaphore()
    for peer in peers:
        pl.semaphore_signal(barrier, inc=1, device_id=peer, device_id_type=MESH)
    pl.semaphore_wait(barrier, len(peers))


def remote(src, dst, sems, at, peer):
    return pltpu.make_async_remote_copy(
        src_ref=src, dst_ref=dst, send_sem=sems.at[0, at], recv_sem=sems.at[1, at],
        device_id=peer, device_id_type=MESH,
    )


def gather_start(axis, count, src, dst, far, near):
    me = lax.axis_index(axis)
    lane, side, lanes = me // 2, me % 2, count // 2
    far_copies = []
    for k in range(1, lanes):
        copy = remote(src, dst.at[me], far, k, {axis: lax.rem(lane + k, lanes) * 2 + side})
        copy.start()
        far_copies.append(copy)
    near_copies = [remote(src, dst.at[me], near, 0, {axis: lane * 2 + 1 - side})]
    near_copies[0].start()
    return far_copies, near_copies


def gather_relay(axis, count, dst, far_copies, near_copies, near):
    me = lax.axis_index(axis)
    lane, side, lanes = me // 2, me % 2, count // 2
    for k in range(1, lanes):
        far_copies[k - 1].wait_recv()
        slot = lax.rem(lane - k + lanes, lanes) * 2 + side
        copy = remote(dst.at[slot], dst.at[slot], near, k, {axis: lane * 2 + 1 - side})
        copy.start()
        near_copies.append(copy)


def gather_end(far_copies, near_copies):
    for copy in far_copies:
        copy.wait_send()
    for copy in near_copies:
        copy.wait()


def spread_kernel(owners, split, weight, picked, cot, all_weight, all_picked, all_cot,
                  wfar, wnear, cfar, cnear, psems, lsems):
    dp, rows = lax.axis_index("dp"), lax.axis_index("rows")
    greet(owners, split)
    wcopies = gather_start("dp", owners, weight, all_weight, wfar, wnear)
    direct = []
    for k in range(1, split):
        to = lax.rem(rows + k, split)
        copy = remote(picked.at[to], all_picked.at[rows], psems, k, {"rows": to})
        copy.start()
        direct.append(copy)
    ccopies = gather_start("rows", split, cot, all_cot, cfar, cnear)
    own = [
        pltpu.make_async_copy(weight, all_weight.at[dp], lsems.at[0]),
        pltpu.make_async_copy(picked.at[rows], all_picked.at[rows], lsems.at[1]),
        pltpu.make_async_copy(cot, all_cot.at[rows], lsems.at[2]),
    ]
    for copy in own:
        copy.start()
    gather_relay("dp", owners, all_weight, *wcopies, wnear)
    gather_relay("rows", split, all_cot, *ccopies, cnear)
    for copy in own + direct:
        copy.wait()
    gather_end(*ccopies)
    gather_end(*wcopies)


def spread(owners, split, weight, picked, cot):
    dma = lambda n: pltpu.SemaphoreType.DMA((2, n))
    return pl.pallas_call(
        functools.partial(spread_kernel, owners, split),
        out_shape=(
            jax.ShapeDtypeStruct((owners,) + weight.shape, weight.dtype),
            jax.ShapeDtypeStruct(picked.shape, picked.dtype),
            jax.ShapeDtypeStruct((split,) + cot.shape, cot.dtype),
        ),
        in_specs=[pl.BlockSpec(memory_space=pl.ANY)] * 3,
        out_specs=[pl.BlockSpec(memory_space=pl.ANY)] * 3,
        scratch_shapes=[
            dma(owners // 2), dma(owners // 2), dma(split // 2), dma(split // 2), dma(split),
            pltpu.SemaphoreType.DMA((3,)),
        ],
        compiler_params=pltpu.CompilerParams(collective_id=1, has_side_effects=True),
        name="spread",
    )(weight, picked, cot)


def combine_kernel(owners, split, sent, conv, small, weight_out, conv_out, small_out,
                   ybuf, zsend, zbuf, sbuf, tbuf, ysems, zsems, csems, ssems, tsems, *gsems):
    dp, rows = lax.axis_index("dp"), lax.axis_index("rows")
    lane, side, lanes = dp // 2, dp % 2, owners // 2
    pair = {"dp": lane * 2 + 1 - side}
    greet(owners, split)
    ycopies = {}
    for c in range(CHUNKS):
        for k in [*range(1, lanes), 0]:
            to = lax.rem(lane + k, lanes)
            copy = remote(sent.at[to * 2 + 1 - side, c], ybuf.at[k, c], ysems, k * CHUNKS + c, pair)
            copy.start()
            ycopies[k, c] = copy
    scopies = []
    sbuf[rows] = small[...]
    for k in range(1, split):
        copy = remote(small, sbuf.at[rows], ssems, k, {"rows": lax.rem(rows + k, split)})
        copy.start()
        scopies.append(copy)
    ccopies = []
    for k in range(1, split):
        to = lax.rem(rows + k, split)
        copy = remote(conv.at[to], conv_out.at[rows], csems, k, {"rows": to})
        copy.start()
        ccopies.append(copy)
    conv_out[rows] = conv[rows]
    zcopies = {}
    tcopies = []
    gathers = []
    for c in range(CHUNKS):
        for k in range(1, lanes):
            to = lax.rem(lane + k, lanes)
            ycopies[k, c].wait_recv()
            zsend[k, c] = (
                sent[to * 2 + side, c].astype(jnp.float32) + ybuf[k, c].astype(jnp.float32)
            ).astype(jnp.bfloat16)
            at = k * CHUNKS + c
            copy = remote(zsend.at[k, c], zbuf.at[k, c], zsems, at, {"dp": to * 2 + side})
            copy.start()
            zcopies[k, c] = copy
        ycopies[0, c].wait_recv()
        if c == 0:
            for copy in scopies:
                copy.wait()
            tbuf[dp] = functools.reduce(jnp.add, [sbuf[i] for i in range(split)])
            for k in range(1, owners):
                copy = remote(tbuf.at[dp], tbuf.at[dp], tsems, k, {"dp": lax.rem(dp + k, owners)})
                copy.start()
                tcopies.append(copy)
    for c in range(CHUNKS):
        total = sent[lane * 2 + side, c].astype(jnp.float32) + ybuf[0, c].astype(jnp.float32)
        for k in range(1, lanes):
            zcopies[k, c].wait_recv()
            total = total + zbuf[k, c].astype(jnp.float32)
        weight_out[c, rows] = total
        dst = weight_out.at[c]
        gathers.append(
            gather_start("rows", split, dst.at[rows], dst, gsems[2 * c], gsems[2 * c + 1])
        )
    for c in range(CHUNKS):
        gather_relay("rows", split, weight_out.at[c], *gathers[c], gsems[2 * c + 1])
    for copy in tcopies + ccopies:
        copy.wait()
    small_out[...] = functools.reduce(jnp.add, [tbuf[i] for i in range(owners)])
    for copy in [*ycopies.values(), *zcopies.values()]:
        copy.wait_send()
    for pieces in gathers:
        gather_end(*pieces)


def combine(owners, split, sent, conv, small):
    lanes = owners // 2
    block = sent.shape[1:]
    dma = lambda n: pltpu.SemaphoreType.DMA((2, n))
    vmem = pl.BlockSpec(memory_space=pltpu.VMEM)
    return pl.pallas_call(
        functools.partial(combine_kernel, owners, split),
        out_shape=(
            jax.ShapeDtypeStruct((CHUNKS, split) + block[1:], jnp.float32),
            jax.ShapeDtypeStruct(conv.shape, conv.dtype),
            jax.ShapeDtypeStruct(small.shape, small.dtype),
        ),
        in_specs=[vmem] * 3,
        out_specs=[vmem] * 3,
        scratch_shapes=[
            pltpu.VMEM((lanes,) + block, jnp.bfloat16),
            pltpu.VMEM((lanes,) + block, jnp.bfloat16),
            pltpu.VMEM((lanes,) + block, jnp.bfloat16),
            pltpu.VMEM((split,) + small.shape, jnp.float32),
            pltpu.VMEM((owners,) + small.shape, jnp.float32),
            dma(lanes * CHUNKS), dma(lanes * CHUNKS), dma(split), dma(split), dma(owners),
        ] + [dma(split // 2)] * (2 * CHUNKS),
        compiler_params=pltpu.CompilerParams(
            collective_id=2, has_side_effects=True, vmem_limit_bytes=VMEM_BYTES
        ),
        name="combine",
    )(sent, conv, small)


def body(candidates, winners, conv_weight, conv_bias, gamma, beta, cotangent):
    images, cand_count, rows_here, width, channels = candidates.shape
    own_rows, out_channels = conv_weight.shape
    split = lax.axis_size("rows")
    owners = lax.axis_size("dp")
    me = lax.axis_index("rows")
    size = channels // GROUPS
    rows_all = rows_here * split
    share = channels // split
    taps = own_rows * owners // channels
    grain = size if own_rows % (split * size) == 0 else math.gcd(own_rows // split, size // split)
    runs = share // grain
    groups_here = GROUPS // split if grain == size else GROUPS
    size_here = share // groups_here
    own_runs = own_rows // (split * grain)
    own_share = own_rows // split
    lined = out_channels if own_share % (16 * CHUNKS) == 0 else 128
    grad_scale = float(images * owners * rows_all * width) ** (-0.5)

    def take(vector):
        return lax.dynamic_index_in_dim(
            vector.reshape(runs, split, grain), me, 1, keepdims=False
        ).reshape(share)

    mine = lax.dynamic_index_in_dim(
        conv_weight.reshape(own_runs, split, grain, out_channels), me, 1, keepdims=False
    ).reshape(-1, lined)

    picked = candidates[:, 0]
    for cand_index in range(1, cand_count):
        picked = jnp.where(
            (winners == cand_index)[:, None, None, None], candidates[:, cand_index], picked
        )
    place = jnp.arange(share)
    flat_picked = picked.reshape(-1, channels)
    sorted_picked = jnp.stack(
        [
            jnp.dot(
                flat_picked,
                (
                    jnp.arange(channels)[:, None]
                    == (place // grain * split + part) * grain + place % grain
                ).astype(jnp.bfloat16),
                preferred_element_type=jnp.float32,
            ).astype(jnp.bfloat16)
            for part in range(split)
        ]
    )
    weight, local, cot = spread(
        owners, split, mine, sorted_picked, cotangent.reshape(-1, out_channels)
    )
    weight = weight.reshape(3, 3, share, out_channels)
    local = local.reshape(split, images, rows_here, width, share)
    local = jnp.swapaxes(local, 0, 1).reshape(images, rows_all, width, share)
    cot = cot.reshape(split, images, rows_here, width, out_channels)
    cot = jnp.swapaxes(cot, 0, 1).reshape(images, rows_all, width, out_channels)

    wide = local.astype(jnp.float32)
    count = rows_all * width * size
    sums = jnp.sum(wide, axis=(1, 2)).reshape(images, groups_here, size_here).sum(axis=2)
    squares = jnp.sum(wide * wide, axis=(1, 2)).reshape(images, groups_here, size_here).sum(axis=2)
    if grain < size:
        sums, squares = lax.psum((sums, squares), "rows")
    mean = sums / count
    inverse = lax.rsqrt(squares / count - mean * mean + EPSILON)
    mean = jnp.repeat(mean, size_here, axis=1)[:, None, None, :]
    inverse = jnp.repeat(inverse, size_here, axis=1)[:, None, None, :]
    normed = (wide - mean) * inverse
    preact = normed * take(gamma) + take(beta)
    sigmoid_pre = jax.nn.sigmoid(preact)
    activated = (preact * sigmoid_pre).astype(jnp.bfloat16)

    padded = jnp.pad(activated, ((0, 0), (1, 1), (1, 1), (0, 0)))
    patches = jnp.concatenate(
        [
            padded[:, a : a + rows_all, b : b + width].reshape(-1, share)
            for a in range(3)
            for b in range(3)
        ],
        axis=1,
    )
    product = lax.dot_general(
        patches, cot.reshape(-1, out_channels), (((0,), (0,)), ((), ())),
        preferred_element_type=jnp.float32,
    )
    sent = (product * grad_scale).astype(jnp.bfloat16).reshape(owners, CHUNKS, -1, lined)

    conv_part = jnp.dot(
        patches, weight.reshape(-1, out_channels), preferred_element_type=jnp.float32
    ).astype(jnp.bfloat16).reshape(images, split, -1, out_channels)
    conv_part = jnp.swapaxes(conv_part, 0, 1)

    flipped = jnp.swapaxes(jnp.flip(weight, (0, 1)), 2, 3)
    back_grad = grad_scale * lax.conv_general_dilated(
        cot, flipped, (1, 1), ((1, 1), (1, 1)),
        dimension_numbers=CONV_DIMS, preferred_element_type=jnp.float32,
    )
    pre_grad = back_grad * sigmoid_pre * (1.0 + preact * (1.0 - sigmoid_pre))
    gamma_term = jnp.sum(pre_grad * normed, axis=(0, 1, 2)).reshape(runs, 1, grain)
    beta_term = jnp.sum(pre_grad, axis=(0, 1, 2)).reshape(runs, 1, grain)
    here = (jnp.arange(split) == me).reshape(1, split, 1)
    gamma_term = jnp.where(here, gamma_term, 0.0).reshape(channels)
    beta_term = jnp.where(here, beta_term, 0.0).reshape(channels)
    bias_term = jnp.sum(cotangent.astype(jnp.float32), axis=(0, 1, 2)) * grad_scale
    small = jnp.concatenate([gamma_term, beta_term, bias_term]).reshape(-1, 128)

    weight_sum, conv_got, small_sum = combine(owners, split, sent, conv_part, small)
    weight_sum = jnp.swapaxes(weight_sum, 0, 1).reshape(split, own_runs, grain, out_channels)
    grad_weight = jnp.swapaxes(weight_sum, 0, 1).reshape(own_rows, out_channels)
    conv_sum = jnp.sum(conv_got.astype(jnp.float32), axis=0).reshape(
        images, rows_here, width, out_channels
    )
    output = (
        conv_sum + conv_bias + picked[..., :out_channels].astype(jnp.float32)
    ).astype(jnp.bfloat16)
    small_sum = small_sum.reshape(-1)
    grad_gamma, grad_beta, grad_bias = (
        small_sum[:channels], small_sum[channels : 2 * channels], small_sum[2 * channels :]
    )
    return (output, grad_weight, grad_bias, grad_gamma, grad_beta)


def solution(mesh):
    in_specs = (
        P("dp", None, "rows", None, None),
        P("dp"),
        P("dp", None),
        P(),
        P(),
        P(),
        P("dp", "rows", None, None),
    )
    out_specs = (P("dp", "rows", None, None), P("dp", None), P(), P(), P())
    return jax.shard_map(body, mesh=mesh, in_specs=in_specs, out_specs=out_specs, check_vma=False)
```

```python
import functools
import math

import jax
import jax.numpy as jnp
from jax import lax
from jax.experimental import pallas as pl
from jax.experimental.pallas import tpu as pltpu
from jax.sharding import PartitionSpec as P

GROUPS = 32


EPSILON = 1e-05


CONV_DIMS = ("NHWC", "HWIO", "NHWC")


CHUNKS = 3


VMEM_BYTES = 48 * 1024 * 1024


MESH = pl.DeviceIdType.MESH


def greet(owners, split):
    dp, rows = lax.axis_index("dp"), lax.axis_index("rows")
    lane, side = dp // 2, dp % 2
    peers = [{"rows": lax.rem(rows + k, split)} for k in range(1, split)]
    peers += [{"dp": lax.rem(dp + k, owners)} for k in range(1, owners)]
    barrier = pltpu.get_barrier_semaphore()
    for peer in peers:
        pl.semaphore_signal(barrier, inc=1, device_id=peer, device_id_type=MESH)
    pl.semaphore_wait(barrier, len(peers))


def remote(src, dst, sems, at, peer):
    return pltpu.make_async_remote_copy(
        src_ref=src, dst_ref=dst, send_sem=sems.at[0, at], recv_sem=sems.at[1, at],
        device_id=peer, device_id_type=MESH,
    )


def gather_start(axis, count, src, dst, far, near):
    me = lax.axis_index(axis)
    lane, side, lanes = me // 2, me % 2, count // 2
    far_copies = []
    for k in range(1, lanes):
        copy = remote(src, dst.at[me], far, k, {axis: lax.rem(lane + k, lanes) * 2 + side})
        copy.start()
        far_copies.append(copy)
    near_copies = [remote(src, dst.at[me], near, 0, {axis: lane * 2 + 1 - side})]
    near_copies[0].start()
    return far_copies, near_copies


def gather_relay(axis, count, dst, far_copies, near_copies, near):
    me = lax.axis_index(axis)
    lane, side, lanes = me // 2, me % 2, count // 2
    for k in range(1, lanes):
        far_copies[k - 1].wait_recv()
        slot = lax.rem(lane - k + lanes, lanes) * 2 + side
        copy = remote(dst.at[slot], dst.at[slot], near, k, {axis: lane * 2 + 1 - side})
        copy.start()
        near_copies.append(copy)


def gather_end(far_copies, near_copies):
    for copy in far_copies:
        copy.wait_send()
    for copy in near_copies:
        copy.wait()


class Part:
    def __init__(self, ref, chunk):
        self.ref, self.chunk = ref, chunk

    @property
    def at(self):
        return self

    def __getitem__(self, slot):
        return self.ref.at[slot, self.chunk]


def spread_kernel(owners, split, weight, picked, cot, all_weight, all_picked, all_cot,
                  cfar, cnear, psems, lsems, *wsems):
    dp, rows = lax.axis_index("dp"), lax.axis_index("rows")
    greet(owners, split)
    parts = [Part(all_weight, c) for c in range(CHUNKS)]
    wcopies = [
        gather_start("dp", owners, weight.at[c], parts[c], wsems[2 * c], wsems[2 * c + 1])
        for c in range(CHUNKS)
    ]
    direct = []
    for k in range(1, split):
        to = lax.rem(rows + k, split)
        copy = remote(picked.at[to], all_picked.at[rows], psems, k, {"rows": to})
        copy.start()
        direct.append(copy)
    ccopies = gather_start("rows", split, cot, all_cot, cfar, cnear)
    own = [
        pltpu.make_async_copy(weight, all_weight.at[dp], lsems.at[0]),
        pltpu.make_async_copy(picked.at[rows], all_picked.at[rows], lsems.at[1]),
        pltpu.make_async_copy(cot, all_cot.at[rows], lsems.at[2]),
    ]
    for copy in own:
        copy.start()
    for c in range(CHUNKS):
        gather_relay("dp", owners, parts[c], *wcopies[c], wsems[2 * c + 1])
        if c == CHUNKS // 2:
            gather_relay("rows", split, all_cot, *ccopies, cnear)
    for copy in own + direct:
        copy.wait()
    gather_end(*ccopies)
    for pieces in wcopies:
        gather_end(*pieces)


def spread(owners, split, weight, picked, cot):
    dma = lambda n: pltpu.SemaphoreType.DMA((2, n))
    return pl.pallas_call(
        functools.partial(spread_kernel, owners, split),
        out_shape=(
            jax.ShapeDtypeStruct((owners,) + weight.shape, weight.dtype),
            jax.ShapeDtypeStruct(picked.shape, picked.dtype),
            jax.ShapeDtypeStruct((split,) + cot.shape, cot.dtype),
        ),
        in_specs=[pl.BlockSpec(memory_space=pl.ANY)] * 3,
        out_specs=[pl.BlockSpec(memory_space=pl.ANY)] * 3,
        scratch_shapes=[
            dma(split // 2), dma(split // 2), dma(split), pltpu.SemaphoreType.DMA((3,)),
        ] + [dma(owners // 2)] * (2 * CHUNKS),
        compiler_params=pltpu.CompilerParams(collective_id=1, has_side_effects=True),
        name="spread",
    )(weight, picked, cot)


def combine_kernel(owners, split, sent, conv, small, weight_out, conv_out, small_out,
                   ybuf, zsend, zbuf, sbuf, tbuf, ysems, zsems, csems, ssems, tsems, *gsems):
    dp, rows = lax.axis_index("dp"), lax.axis_index("rows")
    lane, side, lanes = dp // 2, dp % 2, owners // 2
    pair = {"dp": lane * 2 + 1 - side}
    greet(owners, split)
    ycopies = {}
    for c in range(CHUNKS):
        for k in [*range(1, lanes), 0]:
            to = lax.rem(lane + k, lanes)
            copy = remote(sent.at[to * 2 + 1 - side, c], ybuf.at[k, c], ysems, k * CHUNKS + c, pair)
            copy.start()
            ycopies[k, c] = copy
    scopies = []
    sbuf[rows] = small[...]
    for k in range(1, split):
        copy = remote(small, sbuf.at[rows], ssems, k, {"rows": lax.rem(rows + k, split)})
        copy.start()
        scopies.append(copy)
    ccopies = []
    for k in range(1, split):
        to = lax.rem(rows + k, split)
        copy = remote(conv.at[to], conv_out.at[rows], csems, k, {"rows": to})
        copy.start()
        ccopies.append(copy)
    conv_out[rows] = conv[rows]
    zcopies = {}
    tcopies = []
    gathers = []
    for c in range(CHUNKS):
        for k in range(1, lanes):
            to = lax.rem(lane + k, lanes)
            ycopies[k, c].wait_recv()
            zsend[k, c] = (
                sent[to * 2 + side, c].astype(jnp.float32) + ybuf[k, c].astype(jnp.float32)
            ).astype(jnp.bfloat16)
            at = k * CHUNKS + c
            copy = remote(zsend.at[k, c], zbuf.at[k, c], zsems, at, {"dp": to * 2 + side})
            copy.start()
            zcopies[k, c] = copy
        ycopies[0, c].wait_recv()
        if c == 0:
            for copy in scopies:
                copy.wait()
            tbuf[dp] = functools.reduce(jnp.add, [sbuf[i] for i in range(split)])
            for k in range(1, owners):
                copy = remote(tbuf.at[dp], tbuf.at[dp], tsems, k, {"dp": lax.rem(dp + k, owners)})
                copy.start()
                tcopies.append(copy)
    for c in range(CHUNKS):
        total = sent[lane * 2 + side, c].astype(jnp.float32) + ybuf[0, c].astype(jnp.float32)
        for k in range(1, lanes):
            zcopies[k, c].wait_recv()
            total = total + zbuf[k, c].astype(jnp.float32)
        weight_out[c, rows] = total
        dst = weight_out.at[c]
        gathers.append(
            gather_start("rows", split, dst.at[rows], dst, gsems[2 * c], gsems[2 * c + 1])
        )
    for c in range(CHUNKS):
        gather_relay("rows", split, weight_out.at[c], *gathers[c], gsems[2 * c + 1])
    for copy in tcopies + ccopies:
        copy.wait()
    small_out[...] = functools.reduce(jnp.add, [tbuf[i] for i in range(owners)])
    for copy in [*ycopies.values(), *zcopies.values()]:
        copy.wait_send()
    for pieces in gathers:
        gather_end(*pieces)


def combine(owners, split, sent, conv, small):
    lanes = owners // 2
    block = sent.shape[1:]
    dma = lambda n: pltpu.SemaphoreType.DMA((2, n))
    vmem = pl.BlockSpec(memory_space=pltpu.VMEM)
    return pl.pallas_call(
        functools.partial(combine_kernel, owners, split),
        out_shape=(
            jax.ShapeDtypeStruct((CHUNKS, split) + block[1:], jnp.float32),
            jax.ShapeDtypeStruct(conv.shape, conv.dtype),
            jax.ShapeDtypeStruct(small.shape, small.dtype),
        ),
        in_specs=[vmem] * 3,
        out_specs=[vmem] * 3,
        scratch_shapes=[
            pltpu.VMEM((lanes,) + block, jnp.bfloat16),
            pltpu.VMEM((lanes,) + block, jnp.bfloat16),
            pltpu.VMEM((lanes,) + block, jnp.bfloat16),
            pltpu.VMEM((split,) + small.shape, jnp.float32),
            pltpu.VMEM((owners,) + small.shape, jnp.float32),
            dma(lanes * CHUNKS), dma(lanes * CHUNKS), dma(split), dma(split), dma(owners),
        ] + [dma(split // 2)] * (2 * CHUNKS),
        compiler_params=pltpu.CompilerParams(
            collective_id=2, has_side_effects=True, vmem_limit_bytes=VMEM_BYTES
        ),
        name="combine",
    )(sent, conv, small)


def body(candidates, winners, conv_weight, conv_bias, gamma, beta, cotangent):
    images, cand_count, rows_here, width, channels = candidates.shape
    own_rows, out_channels = conv_weight.shape
    split = lax.axis_size("rows")
    owners = lax.axis_size("dp")
    me = lax.axis_index("rows")
    size = channels // GROUPS
    rows_all = rows_here * split
    share = channels // split
    taps = own_rows * owners // channels
    grain = size if own_rows % (split * size) == 0 else math.gcd(own_rows // split, size // split)
    runs = share // grain
    groups_here = GROUPS // split if grain == size else GROUPS
    size_here = share // groups_here
    own_runs = own_rows // (split * grain)
    own_share = own_rows // split
    lined = out_channels if own_share % (16 * CHUNKS) == 0 else 128
    grad_scale = float(images * owners * rows_all * width) ** (-0.5)

    def take(vector):
        return lax.dynamic_index_in_dim(
            vector.reshape(runs, split, grain), me, 1, keepdims=False
        ).reshape(share)

    mine = lax.dynamic_index_in_dim(
        conv_weight.reshape(own_runs, split, grain, out_channels), me, 1, keepdims=False
    ).reshape(CHUNKS, -1, lined)

    picked = candidates[:, 0]
    for cand_index in range(1, cand_count):
        picked = jnp.where(
            (winners == cand_index)[:, None, None, None], candidates[:, cand_index], picked
        )
    place = jnp.arange(share)
    flat_picked = picked.reshape(-1, channels)
    sorted_picked = jnp.stack(
        [
            jnp.dot(
                flat_picked,
                (
                    jnp.arange(channels)[:, None]
                    == (place // grain * split + part) * grain + place % grain
                ).astype(jnp.bfloat16),
                preferred_element_type=jnp.float32,
            ).astype(jnp.bfloat16)
            for part in range(split)
        ]
    )
    weight, local, cot = spread(
        owners, split, mine, sorted_picked, cotangent.reshape(-1, out_channels)
    )
    weight = weight.reshape(3, 3, share, out_channels)
    local = local.reshape(split, images, rows_here, width, share)
    local = jnp.swapaxes(local, 0, 1).reshape(images, rows_all, width, share)
    cot = cot.reshape(split, images, rows_here, width, out_channels)
    cot = jnp.swapaxes(cot, 0, 1).reshape(images, rows_all, width, out_channels)

    wide = local.astype(jnp.float32)
    count = rows_all * width * size
    sums = jnp.sum(wide, axis=(1, 2)).reshape(images, groups_here, size_here).sum(axis=2)
    squares = jnp.sum(wide * wide, axis=(1, 2)).reshape(images, groups_here, size_here).sum(axis=2)
    if grain < size:
        sums, squares = lax.psum((sums, squares), "rows")
    mean = sums / count
    inverse = lax.rsqrt(squares / count - mean * mean + EPSILON)
    mean = jnp.repeat(mean, size_here, axis=1)[:, None, None, :]
    inverse = jnp.repeat(inverse, size_here, axis=1)[:, None, None, :]
    normed = (wide - mean) * inverse
    preact = normed * take(gamma) + take(beta)
    sigmoid_pre = jax.nn.sigmoid(preact)
    activated = (preact * sigmoid_pre).astype(jnp.bfloat16)

    padded = jnp.pad(activated, ((0, 0), (1, 1), (1, 1), (0, 0)))
    patches = jnp.concatenate(
        [
            padded[:, a : a + rows_all, b : b + width].reshape(-1, share)
            for a in range(3)
            for b in range(3)
        ],
        axis=1,
    )
    product = lax.dot_general(
        patches, cot.reshape(-1, out_channels), (((0,), (0,)), ((), ())),
        preferred_element_type=jnp.float32,
    )
    sent = (product * grad_scale).astype(jnp.bfloat16).reshape(owners, CHUNKS, -1, lined)

    conv_part = jnp.dot(
        patches, weight.reshape(-1, out_channels), preferred_element_type=jnp.float32
    ).astype(jnp.bfloat16).reshape(images, split, -1, out_channels)
    conv_part = jnp.swapaxes(conv_part, 0, 1)

    flipped = jnp.swapaxes(jnp.flip(weight, (0, 1)), 2, 3)
    back_grad = grad_scale * lax.conv_general_dilated(
        cot, flipped, (1, 1), ((1, 1), (1, 1)),
        dimension_numbers=CONV_DIMS, preferred_element_type=jnp.float32,
    )
    pre_grad = back_grad * sigmoid_pre * (1.0 + preact * (1.0 - sigmoid_pre))
    gamma_term = jnp.sum(pre_grad * normed, axis=(0, 1, 2)).reshape(runs, 1, grain)
    beta_term = jnp.sum(pre_grad, axis=(0, 1, 2)).reshape(runs, 1, grain)
    here = (jnp.arange(split) == me).reshape(1, split, 1)
    gamma_term = jnp.where(here, gamma_term, 0.0).reshape(channels)
    beta_term = jnp.where(here, beta_term, 0.0).reshape(channels)
    bias_term = jnp.sum(cotangent.astype(jnp.float32), axis=(0, 1, 2)) * grad_scale
    small = jnp.concatenate([gamma_term, beta_term, bias_term]).reshape(-1, 128)

    weight_sum, conv_got, small_sum = combine(owners, split, sent, conv_part, small)
    weight_sum = jnp.swapaxes(weight_sum, 0, 1).reshape(split, own_runs, grain, out_channels)
    grad_weight = jnp.swapaxes(weight_sum, 0, 1).reshape(own_rows, out_channels)
    conv_sum = jnp.sum(conv_got.astype(jnp.float32), axis=0).reshape(
        images, rows_here, width, out_channels
    )
    output = (
        conv_sum + conv_bias + picked[..., :out_channels].astype(jnp.float32)
    ).astype(jnp.bfloat16)
    small_sum = small_sum.reshape(-1)
    grad_gamma, grad_beta, grad_bias = (
        small_sum[:channels], small_sum[channels : 2 * channels], small_sum[2 * channels :]
    )
    return (output, grad_weight, grad_bias, grad_gamma, grad_beta)


def solution(mesh):
    in_specs = (
        P("dp", None, "rows", None, None),
        P("dp"),
        P("dp", None),
        P(),
        P(),
        P(),
        P("dp", "rows", None, None),
    )
    out_specs = (P("dp", "rows", None, None), P("dp", None), P(), P(), P())
    return jax.shard_map(body, mesh=mesh, in_specs=in_specs, out_specs=out_specs, check_vma=False)
```
